512 devices in a mesh: dp: 64 (over z_lo, x, core), tensor: 8 (over z_hi, y).
Axes of the slice: x: 4, y: 4, z: 16 (z_hi: 2, z_lo: 8; z = z_hi * 8 + z_lo), core: 2. Of those that a mesh axis runs over, the one named last changes fastest.
Arguments:
- language: int32 [64], replicated, may hold values from 0 to 3, as said below
- hidden: bfloat16 [16384, 5632], P('dp', 'tensor'), may hold values from -6 to 6
- context: bfloat16 [16384, 2048], P('dp', 'tensor'), may hold values from -3 to 3
- grad_out: bfloat16 [16384, 4096], P(('dp', 'tensor')), may hold values from -3 to 3
Outputs:
- module_grad: bfloat16 [4, 5632, 4096], P(None, 'tensor', 'dp')
- attention_grad: float32 [4096, 2048], P('dp', 'tensor')
The draws below stay inside these ranges and needn't reach their ends.
Inputs may be any that keep to these rules, and one draw needn't show every extreme that they name: Every language of 0 to 3 belongs to at least one replica; no language has more than 25 replicas.
All inputs are finite; a program needn't handle non-finite values.
Results may differ from the reference program's by a relative error of at most 0.0049.
Values may be sent and summed in bfloat16 or wider, within the bound.
A program may use at most 64 MiB of HBM per device.

```python
import jax
import jax.numpy as jnp
from jax import lax

D = 4096
FF = 5632
HEADS = 16
HD = 128
LANGS = 4
TOK_DEV = 256
TOKENS = 16384
N_DP = 64


def draw_language(key, part):
    key = jax.random.fold_in(key, 11)
    key_cut, key_perm = jax.random.split(key)
    block = 2 * N_DP // LANGS
    pairs = LANGS // 2
    cuts = jax.random.randint(key_cut, (pairs,), block // 4, block - block // 4 + 1)
    position = jnp.arange(N_DP, dtype=jnp.int32)
    pair_index = position // block
    within = position % block
    lang_ids = 2 * pair_index + (within >= jnp.take(cuts, pair_index)).astype(jnp.int32)
    order = jax.random.permutation(key_perm, N_DP)
    return jnp.take(lang_ids, order).astype(jnp.int32)


def raised(result, key, source, target, shards_of, factor):
    def block_of(dim):
        return (jnp.arange(result.shape[dim]) // (result.shape[dim] // shards_of)).reshape((-1,) + (1,) * (result.ndim - 1 - dim))

    one_side = jax.random.permutation(key, shards_of)[block_of(target)]
    other_side = (block_of(target) + shards_of // 2) % shards_of
    return jnp.where((block_of(source) == one_side) | (block_of(source) == other_side), factor * result, result)


def level_of(key, extent, shards, smallest, largest):
    gain = 1.0
    for dim, blocks in shards:
        heights = jax.random.uniform(jax.random.fold_in(jax.random.fold_in(key, 6), dim), (blocks,), jnp.float32, smallest / len(shards), largest / len(shards))
        gain = gain * jnp.repeat(jnp.exp(heights), extent[dim] // blocks).reshape((-1,) + (1,) * (len(extent) - 1 - dim))
    return gain


def scatter_about(stream_key, dims, spread, bound, cuts=(), kind=jnp.bfloat16):
    values = jax.random.normal(stream_key, dims, jnp.float32) * spread
    if len(cuts) > 0:
        values = level_of(stream_key, dims, cuts, -0.22, 0.18) * values
    return jnp.clip(values, min=-bound, max=bound).astype(kind)


def gaussian_with(stream_key, dims, width, most, shards, heavy, kind=jnp.bfloat16):
    drawn = width * jax.random.normal(stream_key, dims, jnp.float32)
    if shards:
        drawn = drawn * level_of(stream_key, dims, shards, -0.22, 0.18)
    return jnp.clip(raised(drawn, jax.random.fold_in(stream_key, 3), *heavy), -most, most).astype(kind)


def setup_inputs(seed: int = 0) -> dict:
    arg_keys = jax.random.split(jax.random.key(seed), 5)
    language = draw_language(jax.random.fold_in(arg_keys[4], 71), 0)
    hidden = scatter_about(arg_keys[1], (TOKENS, FF), 1.0, 6.0, ((0, 64), (1, 8)))
    context = scatter_about(arg_keys[2], (TOKENS, HEADS * HD), 0.2, 3.0, ((0, 64), (1, 8)))
    grad_out = gaussian_with(arg_keys[3], (TOKENS, D), 0.05, 3.0, ((0, 512),), (0, 1, 512, 6.0))
    return {"language": language, "hidden": hidden, "context": context, "grad_out": grad_out}


def reference(language, hidden, context, grad_out):
    hidden_rep = hidden.reshape(N_DP, TOK_DEV, FF)
    grad_rep = grad_out.reshape(N_DP, TOK_DEV, D)

    def add_replica(running, pieces):
        hid_rows, grad_rows, lang_now = pieces
        product = lax.dot_general(hid_rows, grad_rows, (((0,), (0,)), ((), ())), preferred_element_type=jnp.float32)
        product = lax.optimization_barrier(product.astype(jnp.bfloat16)).astype(jnp.float32)
        current = lax.dynamic_index_in_dim(running, lang_now, 0, False)
        running = lax.dynamic_update_index_in_dim(running, current + product, lang_now, 0)
        return running, None

    start = jnp.zeros((LANGS, FF, D), jnp.float32)
    total, _ = lax.scan(add_replica, start, (hidden_rep, grad_rep, language.astype(jnp.int32)))
    module_grad = total.astype(jnp.bfloat16)
    attention_grad = lax.dot_general(grad_out, context, (((0,), (0,)), ((), ())), preferred_element_type=jnp.float32)
    return module_grad, attention_grad
```

```python
import functools

import jax
import jax.numpy as jnp
from jax import lax
from jax.experimental import pallas as pl
from jax.experimental.pallas import tpu as pltpu
from jax.sharding import PartitionSpec as P

LANGS = 4
NX = 4
NC = 2
NH = 2
SUB = 4
BF = jnp.bfloat16
F32 = jnp.float32


def body(nz, ny, lang, hid, ctx, grad, out_m, out_a,
         stage, hext, hraw, hm, gbuf, relay, part, rbuf, obuf,
         ft, ftx, at, atx,
         a_s, a_r, h_s, h_r, hf_s, hf_r, hc_s, hc_r,
         e_s, e_r, ef_s, ef_r, y_s, y_r, g_s, g_r, z_s, z_r, o_s, o_r):
    ff, tok = hid.shape
    nctx = ctx.shape[1]
    fh, ch = ff // 2, nctx // 2
    hr = fh + ch
    rows = LANGS * fh + ch
    tt = grad.shape[0]
    pairs = nz // 2
    sub = rows // SUB
    split = (hr // 32) * 16

    dp = lax.axis_index("dp")
    ten = lax.axis_index("tensor")
    z = dp // (NX * NC)
    x = (dp // NC) % NX
    c = dp % NC
    h = ten // ny
    y = ten % ny
    zp = h * nz + z

    def dev(z_, x_, c_, h_, y_):
        return ((z_ * NX + x_) * NC + c_, h_ * ny + y_)

    def ring(place):
        place = lax.rem(place + 2 * NH * nz, NH * nz)
        return lax.rem(place, nz), place // nz

    def send(src, dst, ssem, rsem, where):
        return pltpu.make_async_remote_copy(
            src_ref=src, dst_ref=dst, send_sem=ssem, recv_sem=rsem,
            device_id=where, device_id_type=pl.DeviceIdType.MESH)

    xr, xl = lax.rem(x + 1, NX), lax.rem(x + NX - 1, NX)
    x2 = lax.rem(x + 2, NX)
    oc = 1 - c
    zu, hu = ring(zp + nz // 2)
    zd, hd = ring(zp - nz // 2)
    zn, zb = lax.rem(z + 1, nz), lax.rem(z + nz - 1, nz)

    barrier = pltpu.get_barrier_semaphore()
    friends = [dev(z, xr, 0, h, y), dev(z, xr, 1, h, y),
               dev(z, xl, 0, h, y), dev(z, xl, 1, h, y),
               dev(z, x2, c, h, y), dev(z, x, oc, h, y),
               dev(zu, x, c, hu, y), dev(zd, x, c, hd, y),
               dev(zn, x, c, h, y), dev(zb, x, c, h, y)]
    for d in range(1, ny):
        friends.append(dev(z, x, c, h, lax.rem(y + d, ny)))
    for f in friends:
        pl.semaphore_signal(barrier, inc=1, device_id=f,
                            device_id_type=pl.DeviceIdType.MESH)

    for k in range(NX):
        for p in range(pairs):
            for i, o in enumerate((nz - 1 - p, p)):
                lo = (o * NX + k) * 128
                stage[k, p, :, i * 128:(i + 1) * 128] = grad[:, lo:lo + 128]
    ctx_t = ctx[...].T
    for k in range(NC):
        hext[k, :fh, :] = hid[k * fh:(k + 1) * fh, :]
        hext[k, fh:, :] = ctx_t[k * ch:(k + 1) * ch, :]
    pl.semaphore_wait(barrier, len(friends))

    a = []
    for d in range(1, NX):
        k = lax.rem(x + d, NX)
        a.append(send(stage.at[k], gbuf.at[:, x, c, ten],
                      a_s.at[d - 1], a_r.at[d - 1], dev(z, k, c, h, y)))
        a[-1].start()
    h1 = []
    for i, k in enumerate((xr, xl)):
        for cc in range(NC):
            h1.append(send(hext.at[cc], hraw.at[x, c],
                           h_s.at[i, cc], h_r.at[i, c], dev(z, k, cc, h, y)))
            h1[-1].start()
    hc = send(hext.at[oc], hraw.at[x, c], hc_s.at[0], hc_r.at[0],
              dev(z, x, oc, h, y))
    hc.start()
    gbuf[:, x, c, ten] = stage[x]
    hraw[x, c] = hext[c]
    for cp in a:
        cp.wait_recv()

    e1, yo, yb = [], [], []
    for p in range(pairs):
        for i, (zz, hh) in enumerate(((zu, hu), (zd, hd))):
            e1.append(send(gbuf.at[p, pl.ds(2 * i, 2), c, ten], relay.at[p, i],
                           e_s.at[p, i], e_r.at[p, i], dev(zz, x, c, hh, y)))
            e1[-1].start()
        for d in range(1, ny):
            blk = gbuf.at[p, :, c, ten]
            yo.append(send(blk, blk, y_s.at[p, 0, d - 1], y_r.at[p, 0, d - 1],
                           dev(z, x, c, h, lax.rem(y + d, ny))))
            yo[-1].start()
    e2 = []
    for p in range(pairs):
        for i, (zz, hh, h0) in enumerate(((zu, hu, hd), (zd, hd, hu))):
            e1[p * 2 + i].wait_recv()
            e2.append(send(relay.at[p, i],
                           gbuf.at[p, pl.ds(2 * i, 2), c, h0 * ny + y],
                           ef_s.at[p, i], ef_r.at[p, i], dev(zz, x, c, hh, y)))
            e2[-1].start()
    h2 = []
    for i, (k, src) in enumerate(((xr, xl), (xl, xr))):
        for cc in range(NC):
            pltpu.make_async_remote_copy(
                src_ref=hext.at[cc], dst_ref=hraw.at[src, cc],
                send_sem=h_s.at[i, cc], recv_sem=h_r.at[i, cc],
                device_id=dev(z, src, cc, h, y),
                device_id_type=pl.DeviceIdType.MESH).wait_recv()
            r0, rn = (0, split) if i == 0 else (split, hr - split)
            blk = hraw.at[src, cc, pl.ds(r0, rn)]
            h2.append(send(blk, blk, hf_s.at[i, cc], hf_r.at[i, cc],
                           dev(z, k, c, h, y)))
            h2[-1].start()
    toth = (1 - h) * ny + y
    for p in range(pairs):
        e2[2 * p].wait_recv()
        e2[2 * p + 1].wait_recv()
        for d in range(1, ny):
            blk = gbuf.at[p, :, c, toth]
            yb.append(send(blk, blk, y_s.at[p, 1, d - 1], y_r.at[p, 1, d - 1],
                           dev(z, x, c, h, lax.rem(y + d, ny))))
            yb[-1].start()

    hc.wait_recv()
    for cp in h2:
        cp.wait_recv()

    def mask_rep(r, carry):
        xs, cs = r // NC, r % NC
        who = lang[z * (NX * NC) + r]
        at_col = pl.ds(pl.multiple_of(r * tok, tok), tok)
        val = hraw[xs, cs, :fh, :]
        for l in range(LANGS):
            keep = jnp.where(who == l, 1.0, 0.0).astype(F32)
            hm[l * fh:(l + 1) * fh, at_col] = (val * keep.astype(BF)).astype(BF)
        hm[LANGS * fh:, at_col] = hraw[xs, cs, fh:, :]
        return carry

    lax.fori_loop(0, NX * NC, mask_rep, 0)

    gc = []
    for p in range(pairs):
        for d in range(ny - 1):
            yo[p * (ny - 1) + d].wait_recv()
            yb[p * (ny - 1) + d].wait_recv()
        blk = gbuf.at[p, :, c]
        gc.append(send(blk, blk, g_s.at[p], g_r.at[p], dev(z, x, oc, h, y)))
        gc[-1].start()

    tile = rows // 3

    def pair(p):
        right = gbuf[p].reshape(NX * NC * tok, 256)

        def some_rows(i, carry):
            r = pl.ds(pl.multiple_of(i * tile, 16), tile)
            res = jnp.dot(hm[r, :], right, preferred_element_type=F32)
            part[nz - 1 - p, r, :] = res[:, :128]
            part[p, r, :] = res[:, 128:]
            return carry

        lax.fori_loop(0, rows // tile, some_rows, 0)

    def hop(way, o, q):
        r = pl.ds(q * sub, sub)
        zz = zn if way == 0 else zb
        return send(obuf.at[o, r], rbuf.at[way, o, r],
                    z_s.at[o, q], z_r.at[way, o, q], dev(zz, x, c, h, y))

    def chain(way, o):
        first = (z == 0) if way == 0 else (z == nz - 1)
        for q in range(SUB):
            r = pl.ds(q * sub, sub)
            cp = hop(way, o, q)

            @pl.when(jnp.logical_not(first))
            def _():
                cp.wait_recv()
                obuf[o, r, :] = (part[o, r, :] + rbuf[way, o, r, :].astype(F32)).astype(BF)

            @pl.when(first)
            def _():
                obuf[o, r, :] = part[o, r, :].astype(BF)

            cp.start()

    def slot(s, last):
        @pl.when(s >= z)
        def _():
            chain(0, nz - 1 + z - s)

        @pl.when(s >= nz - 1 - z)
        def _():
            chain(1, s - (nz - 1) + z)

    for s in range(nz - 1):
        if s < pairs:
            gc[s].wait_recv()
            pair(s)
        slot(s, False)

    for q in range(SUB):
        r = pl.ds(q * sub, sub)

        @pl.when(z > 0)
        def _():
            hop(0, z, q).wait_recv()
            part[z, r, :] = part[z, r, :] + rbuf[0, z, r, :].astype(F32)

        @pl.when(z < nz - 1)
        def _():
            hop(1, z, q).wait_recv()
            part[z, r, :] = part[z, r, :] + rbuf[1, z, r, :].astype(F32)

    for l in range(LANGS):
        ft[l] = part[z, l * fh:(l + 1) * fh, :].T.astype(BF)
    at[...] = part[z, LANGS * fh:, :].T
    mine = pl.ds(pl.multiple_of(c * 64, 64), 64)
    other = pl.ds(pl.multiple_of(oc * 64, 64), 64)
    s1 = send(ft.at[:, other], ftx, o_s.at[0], o_r.at[0], dev(z, x, oc, h, y))
    s2 = send(at.at[other], atx, o_s.at[1], o_r.at[1], dev(z, x, oc, h, y))
    s1.start()
    s2.start()

    for cp in a + h1 + [hc] + e1 + yo + e2 + h2 + yb + gc:
        cp.wait_send()

    def drain(o, carry):
        @pl.when(o != z)
        def _():
            for q in range(SUB):
                hop(0, o, q).wait_send()
        return carry

    lax.fori_loop(0, nz, drain, 0)
    s1.wait()
    s2.wait()
    low = c == 0
    for l in range(LANGS):
        me, it = ft[l, mine, :], ftx[l]
        out_m[l, :, :fh] = jnp.where(low, me, it)
        out_m[l, :, fh:] = jnp.where(low, it, me)
    me, it = at[mine, :], atx[...]
    out_a[:, :ch] = jnp.where(low, me, it)
    out_a[:, ch:] = jnp.where(low, it, me)


def shards(nz, ny, language, hidden, context, grad_out):
    tok, ff = hidden.shape
    nctx = context.shape[1]
    tt = grad_out.shape[0]
    fh, ch = ff // 2, nctx // 2
    hr, rows = fh + ch, LANGS * fh + ch
    pairs = nz // 2
    dma = pltpu.SemaphoreType.DMA
    vm = pl.BlockSpec(memory_space=pltpu.VMEM)
    y1 = max(ny - 1, 1)
    out_m, out_a = pl.pallas_call(
        functools.partial(body, nz, ny),
        out_shape=(jax.ShapeDtypeStruct((LANGS, 64, ff), BF),
                   jax.ShapeDtypeStruct((64, nctx), F32)),
        in_specs=[pl.BlockSpec(memory_space=pltpu.SMEM), vm, vm, vm],
        out_specs=(vm, vm),
        scratch_shapes=[
            pltpu.VMEM((NX, pairs, tt, 256), BF),
            pltpu.VMEM((NC, hr, tok), BF),
            pltpu.VMEM((NX, NC, hr, tok), BF),
            pltpu.VMEM((rows, NX * NC * tok), BF),
            pltpu.VMEM((pairs, NX, NC, NH * ny, tt, 256), BF),
            pltpu.VMEM((pairs, 2, 2, tt, 256), BF),
            pltpu.VMEM((nz, rows, 128), F32),
            pltpu.VMEM((2, nz, rows, 128), BF),
            pltpu.VMEM((nz, rows, 128), BF),
            pltpu.VMEM((LANGS, 128, fh), BF),
            pltpu.VMEM((LANGS, 64, fh), BF),
            pltpu.VMEM((128, ch), F32),
            pltpu.VMEM((64, ch), F32),
            dma((NX - 1,)), dma((NX - 1,)),
            dma((2, NC)), dma((2, NC)), dma((2, NC)), dma((2, NC)),
            dma((1,)), dma((1,)),
            dma((pairs, 2)), dma((pairs, 2)), dma((pairs, 2)), dma((pairs, 2)),
            dma((pairs, 2, y1)), dma((pairs, 2, y1)),
            dma((pairs,)), dma((pairs,)),
            dma((nz, SUB)), dma((2, nz, SUB)),
            dma((2,)), dma((2,)),
        ],
        compiler_params=pltpu.CompilerParams(
            collective_id=0, has_side_effects=True,
            vmem_limit_bytes=48 * 1024 * 1024),
        cost_estimate=pl.CostEstimate(
            flops=2 * rows * NX * NC * tok * nz * 128,
            bytes_accessed=4 * 1024 * 1024, transcendentals=0),
    )(language, hidden.T, context, grad_out)
    return jnp.swapaxes(out_m, 1, 2), out_a


def solution(mesh):
    nz = mesh.shape["dp"] // (NX * NC)
    ny = mesh.shape["tensor"] // NH
    return jax.shard_map(
        functools.partial(shards, nz, ny),
        mesh=mesh,
        in_specs=(P(), P("dp", "tensor"), P("dp", "tensor"), P(("dp", "tensor"), None)),
        out_specs=(P(None, "tensor", "dp"), P("dp", "tensor")),
        check_vma=False,
    )
```

```python
import functools

import jax
import jax.numpy as jnp
from jax import lax
from jax.experimental import pallas as pl
from jax.experimental.pallas import tpu as pltpu
from jax.sharding import PartitionSpec as P

LANGS = 4
NX = 4
NC = 2
NH = 2
BF = jnp.bfloat16
F32 = jnp.float32

ORDERS = {
    4: ("E0 E1 X C0", "E2 C1 M P0", "S0 E3 C2 P1", "S1 C3 P2 S2", "P3 W S3"),
    2: ("E0 X C0 E1", "M P0 S0 C1", "P1 W S1"),
    1: ("E0 X C0 M", "P0 W S0"),
}


def body(nz, ny, lang, hid, ctx, grad, out_m, out_a,
         graw, craw, own, hext, hraw, hm, gbuf, part, rbuf, obuf, fin, sx, acc, om, oa,
         l_s, a_s, a_r, e_s, e_r, h_s, h_r, hf_s, hf_r, hc_s, hc_r,
         y_s, y_r, g_s, g_r, z_s, z_r, f_s, f_r, o_s, o_r, w_s):
    ff, tok = hid.shape
    nctx = ctx.shape[1]
    fh, ch = ff // 2, nctx // 2
    hr = fh + ch
    np_, lp = part.shape[1], part.shape[3]
    pairs = nz // 2
    split = (hr // 32) * 16

    dp = lax.axis_index("dp")
    ten = lax.axis_index("tensor")
    z = dp // (NX * NC)
    x = (dp // NC) % NX
    c = dp % NC
    h = ten // ny
    y = ten % ny
    oc, oh = 1 - c, 1 - h
    toth = oh * ny + y

    def dev(z_, x_, c_, h_, y_):
        return ((z_ * NX + x_) * NC + c_, h_ * ny + y_)

    def send(src, dst, ssem, rsem, where):
        return pltpu.make_async_remote_copy(
            src_ref=src, dst_ref=dst, send_sem=ssem, recv_sem=rsem,
            device_id=where, device_id_type=pl.DeviceIdType.MESH)

    xs_at = [lax.rem(x + d, NX) for d in range(NX)]
    ys_at = [lax.rem(y + d, ny) for d in range(ny)]
    xr, xl = xs_at[1], xs_at[NX - 1]
    zn, zb = lax.rem(z + 1, nz), lax.rem(z + nz - 1, nz)

    barrier = pltpu.get_barrier_semaphore()
    friends = [dev(z, k, c, h, y) for k in xs_at[1:]]
    friends += [dev(z, k, oc, h, y) for k in (x, xr, xl)]
    friends += [dev(z, k, c, oh, y) for k in xs_at]
    friends += [dev(z, x, c, h, k) for k in ys_at[1:]]
    friends += [dev(k, x, cc, h, y) for k in (zn, zb) for cc in range(NC)]
    for f in friends:
        pl.semaphore_signal(barrier, inc=1, device_id=f,
                            device_id_type=pl.DeviceIdType.MESH)

    loads = [pltpu.make_async_copy(grad, graw, l_s.at[0]),
             pltpu.make_async_copy(ctx, craw, l_s.at[1])]
    for k in range(NC):
        loads.append(pltpu.make_async_copy(
            hid.at[pl.ds(k * fh, fh)], hext.at[k, pl.ds(0, fh)], l_s.at[2 + k]))
    for cp in loads:
        cp.start()

    loads[0].wait()
    for p in range(pairs):
        for k in range(NX):
            for i, o in enumerate((nz - 1 - p, p)):
                lo = (o * NX + k) * 128
                own[p, k, :, i * 128:(i + 1) * 128] = graw[:, lo:lo + 128]
    loads[1].wait()
    ctx_t = craw[...].T
    for k in range(NC):
        hext[k, fh:, :] = ctx_t[k * ch:(k + 1) * ch, :]
    loads[2].wait()
    loads[3].wait()
    pl.semaphore_wait(barrier, len(friends))

    e, a, yy = [], [], []

    def start_e(p):
        for d in range(NX):
            e.append((p, send(own.at[p, xs_at[d]], gbuf.at[p, x, c, ten],
                              e_s.at[p, d], e_r.at[p, d], dev(z, xs_at[d], c, oh, y))))
            e[-1][1].start()

    start_e(0)
    for d in range(1, NX):
        a.append(send(own.at[:, xs_at[d]], gbuf.at[:, x, c, ten],
                      a_s.at[d - 1], a_r.at[d - 1], dev(z, xs_at[d], c, h, y)))
        a[-1].start()
    h1 = []
    for i, k in enumerate((xr, xl)):
        for cc in range(NC):
            h1.append(send(hext.at[cc], hraw.at[x, c],
                           h_s.at[i, cc], h_r.at[i, c], dev(z, k, cc, h, y)))
            h1[-1].start()
    hc = send(hext.at[oc], hraw.at[x, c], hc_s.at[0], hc_r.at[0],
              dev(z, x, oc, h, y))
    hc.start()
    for p in range(1, pairs):
        start_e(p)
    gbuf[:, x, c, ten] = own[:, x]
    hraw[x, c] = hext[c]

    def start_y(p, w, t):
        blk = gbuf.at[p, :, c, t]
        for d in range(1, ny):
            yy.append((p, send(blk, blk, y_s.at[p, w, d - 1], y_r.at[p, w, d - 1],
                               dev(z, x, c, h, ys_at[d]))))
            yy[-1][1].start()

    for cp in a:
        cp.wait_recv()
    for p in range(pairs):
        start_y(p, 0, ten)

    def spread_y(p):
        for n, cp in e:
            if n == p:
                cp.wait_recv()
        start_y(p, 1, toth)

    gc = [None] * pairs

    def to_core(p):
        for n, cp in yy:
            if n == p:
                cp.wait_recv()
        blk = gbuf.at[p, :, c]
        gc[p] = send(blk, blk, g_s.at[p], g_r.at[p], dev(z, x, oc, h, y))
        gc[p].start()

    h2 = []

    def on_x():
        for i, (k, src) in enumerate(((xr, xl), (xl, xr))):
            for cc in range(NC):
                send(hext.at[cc], hraw.at[src, cc], h_s.at[i, cc], h_r.at[i, cc],
                     dev(z, src, cc, h, y)).wait_recv()
                r0, rn = (0, split) if i == 0 else (split, hr - split)
                blk = hraw.at[src, cc, pl.ds(r0, rn)]
                h2.append(send(blk, blk, hf_s.at[i, cc], hf_r.at[i, cc],
                               dev(z, k, c, h, y)))
                h2[-1].start()

    def mask_rep(r, carry):
        xs, cs = r // NC, r % NC
        who = lang[z * (NX * NC) + r]
        at_col = pl.ds(pl.multiple_of(r * tok, tok), tok)
        val = hraw[xs, cs, :fh, :]
        for l in range(LANGS):
            keep = jnp.where(who == l, 1.0, 0.0).astype(F32)
            hm[l * fh:(l + 1) * fh, at_col] = (val * keep.astype(BF)).astype(BF)
        hm[LANGS * fh:, at_col] = hraw[xs, cs, fh:, :]
        return carry

    def masked():
        hc.wait_recv()
        for cp in h2:
            cp.wait_recv()
        lax.fori_loop(0, NX * NC, mask_rep, 0)

    def pair(p):
        gc[p].wait_recv()
        right = gbuf[p].reshape(NX * NC * tok, 256)

        def some_rows(i, carry):
            r = pl.ds(pl.multiple_of(i * lp, lp), lp)
            res = jnp.dot(hm[r, :], right, preferred_element_type=F32).T
            part[nz - 1 - p, i] = res[:128]
            part[p, i] = res[128:]
            return carry

        lax.fori_loop(0, np_, some_rows, 0)

    def hop(way, o, q):
        return send(obuf.at[o, q], rbuf.at[way, o, q],
                    z_s.at[o, q], z_r.at[way, o, q],
                    dev(zn if way == 0 else zb, x, c, h, y))

    def last_hop(way, q, cc, o, cs):
        return send(obuf.at[o, q, pl.ds(64 * cc, 64)], fin.at[way, cs, q],
                    f_s.at[way, q, cc], f_r.at[way, q, cs],
                    dev(zn if way == 0 else zb, x, cc, h, y))

    def chain(way, o):
        first = (z == 0) if way == 0 else (z == nz - 1)
        last = (o == z + 1) if way == 0 else (o == z - 1)
        for q in range(np_):
            @pl.when(jnp.logical_not(first))
            def _():
                hop(way, o, q).wait_recv()
                obuf[o, q] = (part[o, q] + rbuf[way, o, q].astype(F32)).astype(BF)

            @pl.when(first)
            def _():
                obuf[o, q] = part[o, q].astype(BF)

            @pl.when(last)
            def _():
                for cc in range(NC):
                    last_hop(way, q, cc, o, c).start()

            @pl.when(jnp.logical_not(last))
            def _():
                hop(way, o, q).start()

    def slot(s):
        @pl.when(s >= z)
        def _():
            chain(0, nz - 1 + z - s)

        @pl.when(s >= nz - 1 - z)
        def _():
            chain(1, s - (nz - 1) + z)

    mine = pl.ds(pl.multiple_of(c * 64, 64), 64)
    other = pl.ds(pl.multiple_of(oc * 64, 64), 64)
    swap = send(part.at[z, :, other], sx, o_s.at[0], o_r.at[0], dev(z, x, oc, h, y))

    do = {"E": spread_y, "C": to_core, "X": on_x, "M": masked,
          "P": pair, "S": slot, "W": swap.start}
    for step in [w for group in ORDERS[pairs] for w in group.split()]:
        do[step[0]](*(int(v) for v in step[1:]))
    for s in range(pairs, nz - 1):
        slot(s)

    for cp in a + h1 + [hc] + h2 + gc:
        cp.wait_send()
    for n, cp in e + yy:
        cp.wait_send()

    swap.wait()
    low = c == 0
    writes = []
    for q in range(np_):
        one, two = part[z, q, mine, :], sx[q]
        acc[0, :, q * lp:(q + 1) * lp] = jnp.where(low, one, two)
        acc[1, :, q * lp:(q + 1) * lp] = jnp.where(low, two, one)
        for way, there in ((0, z > 0), (1, z < nz - 1)):
            @pl.when(there)
            def _():
                for cs in range(NC):
                    last_hop(way, q, cs, z, cs).wait_recv()
                    at_l = slice(q * lp, (q + 1) * lp)
                    acc[cs, :, at_l] = acc[cs, :, at_l] + fin[way, cs, q].astype(F32)

        for l in range(LANGS):
            if q * lp < (l + 1) * fh <= (q + 1) * lp:
                for cs in range(NC):
                    om[l, :, cs * fh:(cs + 1) * fh] = acc[cs, :, l * fh:(l + 1) * fh].astype(BF)
                writes.append(pltpu.make_async_copy(om.at[l], out_m.at[l], w_s.at[l]))
                writes[-1].start()
    for cs in range(NC):
        oa[:, cs * ch:(cs + 1) * ch] = acc[cs, :, LANGS * fh:]
    writes.append(pltpu.make_async_copy(oa, out_a, w_s.at[LANGS]))
    writes[-1].start()

    def drain(o, carry):
        @pl.when(jnp.logical_or(o > z + 1, o < z - 1))
        def _():
            for q in range(np_):
                hop(0, o, q).wait_send()
        return carry

    lax.fori_loop(0, nz, drain, 0)
    for q in range(np_):
        for way, there in ((0, z < nz - 1), (1, z > 0)):
            @pl.when(there)
            def _():
                for cc in range(NC):
                    last_hop(way, q, cc, z, c).wait_send()
    for cp in writes:
        cp.wait()


def shards(nz, ny, language, hidden, context, grad_out):
    tok, ff = hidden.shape
    nctx = context.shape[1]
    tt = grad_out.shape[0]
    fh, ch = ff // 2, nctx // 2
    hr, rows = fh + ch, LANGS * fh + ch
    np_ = 4 if rows % 512 == 0 else 3
    lp = rows // np_
    pairs = nz // 2
    dma = pltpu.SemaphoreType.DMA
    hbm = pl.BlockSpec(memory_space=pltpu.HBM)
    y1 = max(ny - 1, 1)
    out_m, out_a = pl.pallas_call(
        functools.partial(body, nz, ny),
        out_shape=(jax.ShapeDtypeStruct((LANGS, 64, ff), BF),
                   jax.ShapeDtypeStruct((64, nctx), F32)),
        in_specs=[pl.BlockSpec(memory_space=pltpu.SMEM), hbm, hbm, hbm],
        out_specs=(hbm, hbm),
        scratch_shapes=[
            pltpu.VMEM((tt, nz * NX * 128), BF),
            pltpu.VMEM((tok, nctx), BF),
            pltpu.VMEM((pairs, NX, tt, 256), BF),
            pltpu.VMEM((NC, hr, tok), BF),
            pltpu.VMEM((NX, NC, hr, tok), BF),
            pltpu.VMEM((rows, NX * NC * tok), BF),
            pltpu.VMEM((pairs, NX, NC, NH * ny, tt, 256), BF),
            pltpu.VMEM((nz, np_, 128, lp), F32),
            pltpu.VMEM((2, nz, np_, 128, lp), BF),
            pltpu.VMEM((nz, np_, 128, lp), BF),
            pltpu.VMEM((2, NC, np_, 64, lp), BF),
            pltpu.VMEM((np_, 64, lp), F32),
            pltpu.VMEM((NC, 64, rows), F32),
            pltpu.VMEM((LANGS, 64, ff), BF),
            pltpu.VMEM((64, nctx), F32),
            dma((2 + NC,)),
            dma((NX - 1,)), dma((NX - 1,)),
            dma((pairs, NX)), dma((pairs, NX)),
            dma((2, NC)), dma((2, NC)), dma((2, NC)), dma((2, NC)),
            dma((1,)), dma((1,)),
            dma((pairs, 2, y1)), dma((pairs, 2, y1)),
            dma((pairs,)), dma((pairs,)),
            dma((nz, np_)), dma((2, nz, np_)),
            dma((2, np_, NC)), dma((2, np_, NC)),
            dma((1,)), dma((1,)),
            dma((1 + LANGS,)),
        ],
        compiler_params=pltpu.CompilerParams(
            collective_id=0, has_side_effects=True,
            vmem_limit_bytes=60 * 1024 * 1024),
        cost_estimate=pl.CostEstimate(
            flops=2 * rows * NX * NC * tok * nz * 128,
            bytes_accessed=4 * 1024 * 1024, transcendentals=0),
    )(language, hidden.T, context, grad_out)
    return jnp.swapaxes(out_m, 1, 2), out_a


def solution(mesh):
    nz = mesh.shape["dp"] // (NX * NC)
    ny = mesh.shape["tensor"] // NH
    return jax.shard_map(
        functools.partial(shards, nz, ny),
        mesh=mesh,
        in_specs=(P(), P("dp", "tensor"), P("dp", "tensor"), P(("dp", "tensor"), None)),
        out_specs=(P(None, "tensor", "dp"), P("dp", "tensor")),
        check_vma=False,
    )
```

```python
import functools

import jax
import jax.numpy as jnp
from jax import lax
from jax.experimental import pallas as pl
from jax.experimental.pallas import tpu as pltpu
from jax.sharding import PartitionSpec as P

LANGS = 4
NX = 4
NC = 2
NH = 2
BF = jnp.bfloat16
F32 = jnp.float32

ORDERS = {
    4: (4, 4, "X M E0 E1", "C0 N E2 C1", "P0 E3 C2 P1", "S1 C3 P2 S2", "P3 W S3"),
    2: (1, 1, "E0 X K1 Y1", "C0 M N P0", "E1 C1 P1 W", "S1"),
    1: (1, 1, "E0 X C0 M", "N P0 W"),
}


def body(nz, ny, lang, hid, ctx, grad, out_m, out_a,
         graw, craw, own, hext, hraw, hm, gbuf, part, rbuf, obuf, fin, sx, acc, om, oa,
         l_s, a_s, a_r, e_s, e_r, h_s, h_r, hf_s, hf_r, hc_s, hc_r,
         y_s, y_r, g_s, g_r, z_s, z_r, f_s, f_r, o_s, o_r, w_s):
    ff, tok = hid.shape
    nctx = ctx.shape[1]
    fh, ch = ff // 2, nctx // 2
    hr = fh + ch
    np_, lp = part.shape[1], part.shape[3]
    pairs = nz // 2
    split = (hr // 32) * 16

    dp = lax.axis_index("dp")
    ten = lax.axis_index("tensor")
    z = dp // (NX * NC)
    x = (dp // NC) % NX
    c = dp % NC
    h = ten // ny
    y = ten % ny
    oc, oh = 1 - c, 1 - h
    toth = oh * ny + y

    def dev(z_, x_, c_, h_, y_):
        return ((z_ * NX + x_) * NC + c_, h_ * ny + y_)

    def send(src, dst, ssem, rsem, where):
        return pltpu.make_async_remote_copy(
            src_ref=src, dst_ref=dst, send_sem=ssem, recv_sem=rsem,
            device_id=where, device_id_type=pl.DeviceIdType.MESH)

    xs_at = [lax.rem(x + d, NX) for d in range(NX)]
    ys_at = [lax.rem(y + d, ny) for d in range(ny)]
    xr, xl = xs_at[1], xs_at[NX - 1]
    zn, zb = lax.rem(z + 1, nz), lax.rem(z + nz - 1, nz)

    loads = [pltpu.make_async_copy(grad, graw, l_s.at[0]),
             pltpu.make_async_copy(ctx, craw, l_s.at[1])]
    for k in range(NC):
        loads.append(pltpu.make_async_copy(
            hid.at[pl.ds(k * fh, fh)], hext.at[k, pl.ds(0, fh)], l_s.at[2 + k]))
    for cp in loads:
        cp.start()

    barrier = pltpu.get_barrier_semaphore()
    friends = [dev(z, k, c, h, y) for k in xs_at[1:]]
    friends += [dev(z, k, oc, h, y) for k in (x, xr, xl)]
    friends += [dev(z, k, c, oh, y) for k in xs_at]
    friends += [dev(z, x, c, h, k) for k in ys_at[1:]]
    friends += [dev(k, x, cc, h, y) for k in (zn, zb) for cc in range(NC)]
    for f in friends:
        pl.semaphore_signal(barrier, inc=1, device_id=f,
                            device_id_type=pl.DeviceIdType.MESH)

    loads[0].wait()
    for p in range(pairs):
        for k in range(NX):
            for i, o in enumerate((nz - 1 - p, p)):
                lo = (o * NX + k) * 128
                own[p, k, :, i * 128:(i + 1) * 128] = graw[:, lo:lo + 128]
    pl.semaphore_wait(barrier, len(friends))

    e, a, yy = [], [], []

    def start_e(p):
        for d in range(NX):
            e.append((p, send(own.at[p, xs_at[d]], gbuf.at[p, x, c, ten],
                              e_s.at[p, d], e_r.at[p, d], dev(z, xs_at[d], c, oh, y))))
            e[-1][1].start()

    order = ORDERS[pairs]
    for p in range(order[0]):
        start_e(p)
    for d in range(1, NX):
        a.append(send(own.at[:, xs_at[d]], gbuf.at[:, x, c, ten],
                      a_s.at[d - 1], a_r.at[d - 1], dev(z, xs_at[d], c, h, y)))
        a[-1].start()
    loads[1].wait()
    ctx_t = craw[...].T
    for k in range(NC):
        hext[k, fh:, :] = ctx_t[k * ch:(k + 1) * ch, :]
    loads[2].wait()
    loads[3].wait()
    h1 = []
    for i, k in enumerate((xr, xl)):
        for cc in range(NC):
            h1.append(send(hext.at[cc], hraw.at[x, c],
                           h_s.at[i, cc], h_r.at[i, c], dev(z, k, cc, h, y)))
            h1[-1].start()
    hc = send(hext.at[oc], hraw.at[x, c], hc_s.at[0], hc_r.at[0],
              dev(z, x, oc, h, y))
    hc.start()
    gbuf[:, x, c, ten] = own[:, x]
    hraw[x, c] = hext[c]

    def start_y(p, w, t):
        blk = gbuf.at[p, :, c, t]
        for d in range(1, ny):
            yy.append((p, send(blk, blk, y_s.at[p, w, d - 1], y_r.at[p, w, d - 1],
                               dev(z, x, c, h, ys_at[d]))))
            yy[-1][1].start()

    for cp in a:
        cp.wait_recv()
    for p in range(order[1]):
        start_y(p, 0, ten)

    def spread_y(p):
        for n, cp in e:
            if n == p:
                cp.wait_recv()
        start_y(p, 1, toth)

    gc = [None] * pairs

    def to_core(p):
        for n, cp in yy:
            if n == p:
                cp.wait_recv()
        blk = gbuf.at[p, :, c]
        gc[p] = send(blk, blk, g_s.at[p], g_r.at[p], dev(z, x, oc, h, y))
        gc[p].start()

    h2 = []

    def on_x():
        for i, (k, src) in enumerate(((xr, xl), (xl, xr))):
            for cc in range(NC):
                send(hext.at[cc], hraw.at[src, cc], h_s.at[i, cc], h_r.at[i, cc],
                     dev(z, src, cc, h, y)).wait_recv()
                r0, rn = (0, split) if i == 0 else (split, hr - split)
                blk = hraw.at[src, cc, pl.ds(r0, rn)]
                h2.append(send(blk, blk, hf_s.at[i, cc], hf_r.at[i, cc],
                               dev(z, k, c, h, y)))
                h2[-1].start()

    def mask_rep(xs, cs):
        r = xs * NC + cs
        who = lang[z * (NX * NC) + r]
        at_col = pl.ds(pl.multiple_of(r * tok, tok), tok)
        val = hraw[xs, cs, :fh, :]
        for l in range(LANGS):
            keep = jnp.where(who == l, 1.0, 0.0).astype(F32)
            hm[l * fh:(l + 1) * fh, at_col] = (val * keep.astype(BF)).astype(BF)
        hm[LANGS * fh:, at_col] = hraw[xs, cs, fh:, :]

    def mask_near():
        hc.wait_recv()

        def some(i, carry):
            mask_rep(lax.rem(x + (NX - 1) + i // NC, NX), i % NC)
            return carry

        lax.fori_loop(0, (NX - 1) * NC, some, 0)

    def mask_far():
        for cp in h2:
            cp.wait_recv()
        for cs in range(NC):
            mask_rep(xs_at[2], cs)

    def pair(p):
        gc[p].wait_recv()
        right = gbuf[p].reshape(NX * NC * tok, 256)

        def some_rows(i, carry):
            r = pl.ds(pl.multiple_of(i * lp, lp), lp)
            res = jnp.dot(hm[r, :], right, preferred_element_type=F32).T
            part[nz - 1 - p, i] = res[:128]
            part[p, i] = res[128:]
            if p == 0:
                @pl.when(z == 0)
                def _():
                    chain_piece(0, nz - 1, i)

                @pl.when(z == nz - 1)
                def _():
                    chain_piece(1, 0, i)
            return carry

        lax.fori_loop(0, np_, some_rows, 0)

    def hop(way, o, q):
        return send(obuf.at[o, q], rbuf.at[way, o, q],
                    z_s.at[o, q], z_r.at[way, o, q],
                    dev(zn if way == 0 else zb, x, c, h, y))

    def last_hop(way, q, cc, o, cs):
        return send(obuf.at[o, q, pl.ds(64 * cc, 64)], fin.at[way, cs, q],
                    f_s.at[way, q, cc], f_r.at[way, q, cs],
                    dev(zn if way == 0 else zb, x, cc, h, y))

    def chain_piece(way, o, q):
        first = (z == 0) if way == 0 else (z == nz - 1)
        last = (o == z + 1) if way == 0 else (o == z - 1)

        @pl.when(jnp.logical_not(first))
        def _():
            hop(way, o, q).wait_recv()
            obuf[o, q] = (part[o, q] + rbuf[way, o, q].astype(F32)).astype(BF)

        @pl.when(first)
        def _():
            obuf[o, q] = part[o, q].astype(BF)

        @pl.when(last)
        def _():
            for cc in range(NC):
                last_hop(way, q, cc, o, c).start()

        @pl.when(jnp.logical_not(last))
        def _():
            hop(way, o, q).start()

    def slot(s):
        @pl.when(s >= z)
        def _():
            for q in range(np_):
                chain_piece(0, nz - 1 + z - s, q)

        @pl.when(s >= nz - 1 - z)
        def _():
            for q in range(np_):
                chain_piece(1, s - (nz - 1) + z, q)

    mine = pl.ds(pl.multiple_of(c * 64, 64), 64)
    other = pl.ds(pl.multiple_of(oc * 64, 64), 64)
    swap = send(part.at[z, :, other], sx, o_s.at[0], o_r.at[0], dev(z, x, oc, h, y))

    do = {"K": start_e, "Y": lambda p: start_y(p, 0, ten), "E": spread_y, "C": to_core, "X": on_x, "M": mask_near, "N": mask_far,
          "P": pair, "S": slot, "W": swap.start}
    for step in [w for group in order[2:] for w in group.split()]:
        do[step[0]](*(int(v) for v in step[1:]))
    for s in range(max(pairs, 1), nz - 1):
        slot(s)

    for cp in a + h1 + [hc] + h2 + gc:
        cp.wait_send()
    for n, cp in e + yy:
        cp.wait_send()

    swap.wait()
    low = c == 0
    writes = []
    for q in range(np_):
        one, two = part[z, q, mine, :], sx[q]
        acc[0, :, q * lp:(q + 1) * lp] = jnp.where(low, one, two)
        acc[1, :, q * lp:(q + 1) * lp] = jnp.where(low, two, one)
        for way, there in ((0, z > 0), (1, z < nz - 1)):
            @pl.when(there)
            def _():
                for cs in range(NC):
                    last_hop(way, q, cs, z, cs).wait_recv()
                    at_l = slice(q * lp, (q + 1) * lp)
                    acc[cs, :, at_l] = acc[cs, :, at_l] + fin[way, cs, q].astype(F32)

        for l in range(LANGS):
            if q * lp < (l + 1) * fh <= (q + 1) * lp:
                for cs in range(NC):
                    om[l, :, cs * fh:(cs + 1) * fh] = acc[cs, :, l * fh:(l + 1) * fh].astype(BF)
                writes.append(pltpu.make_async_copy(om.at[l], out_m.at[l], w_s.at[l]))
                writes[-1].start()
    for cs in range(NC):
        oa[:, cs * ch:(cs + 1) * ch] = acc[cs, :, LANGS * fh:]
    writes.append(pltpu.make_async_copy(oa, out_a, w_s.at[LANGS]))
    writes[-1].start()

    def drain(o, carry):
        @pl.when(jnp.logical_or(o > z + 1, o < z - 1))
        def _():
            for q in range(np_):
                hop(0, o, q).wait_send()
        return carry

    lax.fori_loop(0, nz, drain, 0)
    for q in range(np_):
        for way, there in ((0, z < nz - 1), (1, z > 0)):
            @pl.when(there)
            def _():
                for cc in range(NC):
                    last_hop(way, q, cc, z, c).wait_send()
    for cp in writes:
        cp.wait()


def shards(nz, ny, language, hidden, context, grad_out):
    tok, ff = hidden.shape
    nctx = context.shape[1]
    tt = grad_out.shape[0]
    fh, ch = ff // 2, nctx // 2
    hr, rows = fh + ch, LANGS * fh + ch
    np_ = 4 if rows % 512 == 0 else 3
    lp = rows // np_
    pairs = nz // 2
    dma = pltpu.SemaphoreType.DMA
    hbm = pl.BlockSpec(memory_space=pltpu.HBM)
    y1 = max(ny - 1, 1)
    out_m, out_a = pl.pallas_call(
        functools.partial(body, nz, ny),
        out_shape=(jax.ShapeDtypeStruct((LANGS, 64, ff), BF),
                   jax.ShapeDtypeStruct((64, nctx), F32)),
        in_specs=[pl.BlockSpec(memory_space=pltpu.SMEM), hbm, hbm, hbm],
        out_specs=(hbm, hbm),
        scratch_shapes=[
            pltpu.VMEM((tt, nz * NX * 128), BF),
            pltpu.VMEM((tok, nctx), BF),
            pltpu.VMEM((pairs, NX, tt, 256), BF),
            pltpu.VMEM((NC, hr, tok), BF),
            pltpu.VMEM((NX, NC, hr, tok), BF),
            pltpu.VMEM((rows, NX * NC * tok), BF),
            pltpu.VMEM((pairs, NX, NC, NH * ny, tt, 256), BF),
            pltpu.VMEM((nz, np_, 128, lp), F32),
            pltpu.VMEM((2, nz, np_, 128, lp), BF),
            pltpu.VMEM((nz, np_, 128, lp), BF),
            pltpu.VMEM((2, NC, np_, 64, lp), BF),
            pltpu.VMEM((np_, 64, lp), F32),
            pltpu.VMEM((NC, 64, rows), F32),
            pltpu.VMEM((LANGS, 64, ff), BF),
            pltpu.VMEM((64, nctx), F32),
            dma((2 + NC,)),
            dma((NX - 1,)), dma((NX - 1,)),
            dma((pairs, NX)), dma((pairs, NX)),
            dma((2, NC)), dma((2, NC)), dma((2, NC)), dma((2, NC)),
            dma((1,)), dma((1,)),
            dma((pairs, 2, y1)), dma((pairs, 2, y1)),
            dma((pairs,)), dma((pairs,)),
            dma((nz, np_)), dma((2, nz, np_)),
            dma((2, np_, NC)), dma((2, np_, NC)),
            dma((1,)), dma((1,)),
            dma((1 + LANGS,)),
        ],
        compiler_params=pltpu.CompilerParams(
            collective_id=0, has_side_effects=True,
            vmem_limit_bytes=60 * 1024 * 1024),
        cost_estimate=pl.CostEstimate(
            flops=2 * rows * NX * NC * tok * nz * 128,
            bytes_accessed=4 * 1024 * 1024, transcendentals=0),
    )(language, hidden.T, context, grad_out)
    return jnp.swapaxes(out_m, 1, 2), out_a


def solution(mesh):
    nz = mesh.shape["dp"] // (NX * NC)
    ny = mesh.shape["tensor"] // NH
    return jax.shard_map(
        functools.partial(shards, nz, ny),
        mesh=mesh,
        in_specs=(P(), P("dp", "tensor"), P("dp", "tensor"), P(("dp", "tensor"), None)),
        out_specs=(P(None, "tensor", "dp"), P("dp", "tensor")),
        check_vma=False,
    )
```

```python
import functools

import jax
import jax.numpy as jnp
from jax import lax
from jax.experimental import pallas as pl
from jax.experimental.pallas import tpu as pltpu
from jax.sharding import PartitionSpec as P

LANGS = 4
NX = 4
NC = 2
NH = 2
BF = jnp.bfloat16
F32 = jnp.float32

ORDERS = {
    4: (4, 4, "F0 F1 F2 F3", "X M E0 E1", "C0 N E2 C1", "P0 E3 C2 P1", "S1 C3 P2 S2", "P3 W S3"),
    2: (1, 1, "E0 X K1 Y1", "C0 M N P0", "E1 C1 P1 W", "S1"),
    1: (1, 1, "E0 X C0 M", "N P0 W"),
}


def body(nz, ny, lang, hid, ctx, grad, out_m, out_a,
         graw, craw, own, hext, hraw, hm, gbuf, part, rbuf, obuf, fin, sx, acc, om, oa,
         l_s, a_s, a_r, e_s, e_r, h_s, h_r, hf_s, hf_r, hc_s, hc_r,
         y_s, y_r, g_s, g_r, z_s, z_r, f_s, f_r, o_s, o_r, w_s):
    ff, tok = hid.shape
    nctx = ctx.shape[1]
    fh, ch = ff // 2, nctx // 2
    hr = fh + ch
    np_, lp = part.shape[1], part.shape[3]
    pairs = nz // 2
    split = (hr // 32) * 16

    dp = lax.axis_index("dp")
    ten = lax.axis_index("tensor")
    z = dp // (NX * NC)
    x = (dp // NC) % NX
    c = dp % NC
    h = ten // ny
    y = ten % ny
    oc, oh = 1 - c, 1 - h
    toth = oh * ny + y

    def dev(z_, x_, c_, h_, y_):
        return ((z_ * NX + x_) * NC + c_, h_ * ny + y_)

    def send(src, dst, ssem, rsem, where):
        return pltpu.make_async_remote_copy(
            src_ref=src, dst_ref=dst, send_sem=ssem, recv_sem=rsem,
            device_id=where, device_id_type=pl.DeviceIdType.MESH)

    xs_at = [lax.rem(x + d, NX) for d in range(NX)]
    ys_at = [lax.rem(y + d, ny) for d in range(ny)]
    xr, xl = xs_at[1], xs_at[NX - 1]
    zn, zb = lax.rem(z + 1, nz), lax.rem(z + nz - 1, nz)

    loads = [pltpu.make_async_copy(grad, graw, l_s.at[0]),
             pltpu.make_async_copy(ctx, craw, l_s.at[1])]
    for k in range(NC):
        loads.append(pltpu.make_async_copy(
            hid.at[pl.ds(k * fh, fh)], hext.at[k, pl.ds(0, fh)], l_s.at[2 + k]))
    for cp in loads:
        cp.start()

    barrier = pltpu.get_barrier_semaphore()
    friends = [dev(z, k, c, h, y) for k in xs_at[1:]]
    friends += [dev(z, k, oc, h, y) for k in (x, xr, xl)]
    friends += [dev(z, k, c, oh, y) for k in xs_at]
    friends += [dev(z, x, c, h, k) for k in ys_at[1:]]
    friends += [dev(k, x, cc, h, y) for k in (zn, zb) for cc in range(NC)]
    for f in friends:
        pl.semaphore_signal(barrier, inc=1, device_id=f,
                            device_id_type=pl.DeviceIdType.MESH)

    loads[0].wait()
    for p in range(pairs):
        for k in range(NX):
            for i, o in enumerate((nz - 1 - p, p)):
                lo = (o * NX + k) * 128
                own[p, k, :, i * 128:(i + 1) * 128] = graw[:, lo:lo + 128]
    pl.semaphore_wait(barrier, len(friends))

    e, a, yy, yo = [], [], [], []

    def start_e(p):
        for d in range(NX):
            e.append((p, send(own.at[p, xs_at[d]], gbuf.at[p, x, c, ten],
                              e_s.at[p, d], e_r.at[p, d], dev(z, xs_at[d], c, oh, y))))
            e[-1][1].start()

    order = ORDERS[pairs]
    for p in range(order[0]):
        start_e(p)
    for d in range(1, NX):
        a.append(send(own.at[:, xs_at[d]], gbuf.at[:, x, c, ten],
                      a_s.at[d - 1], a_r.at[d - 1], dev(z, xs_at[d], c, h, y)))
        a[-1].start()
    loads[1].wait()
    ctx_t = craw[...].T
    for k in range(NC):
        hext[k, fh:, :] = ctx_t[k * ch:(k + 1) * ch, :]
    loads[2].wait()
    loads[3].wait()
    h1 = []
    for i, k in enumerate((xr, xl)):
        for cc in range(NC):
            h1.append(send(hext.at[cc], hraw.at[x, c],
                           h_s.at[i, cc], h_r.at[i, c], dev(z, k, cc, h, y)))
            h1[-1].start()
    hc = send(hext.at[oc], hraw.at[x, c], hc_s.at[0], hc_r.at[0],
              dev(z, x, oc, h, y))
    hc.start()
    gbuf[:, x, c, ten] = own[:, x]
    hraw[x, c] = hext[c]

    def start_y(p, w, t):
        blk = gbuf.at[p, :, c, t]
        for d in range(1, ny):
            if w == 0 and ny == 4 and d == 2:
                continue
            (yo if w == 0 and ny == 4 else yy).append((p, send(blk, blk, y_s.at[p, w, d - 1], y_r.at[p, w, d - 1],
                               dev(z, x, c, h, ys_at[d]))))
            (yo if w == 0 and ny == 4 else yy)[-1][1].start()

    def on_y(p):
        for n, cp in yo:
            if n == p:
                cp.wait_recv()
        for i, (to, src) in enumerate(((1, 3), (3, 1))):
            blk = gbuf.at[p, pl.ds(2 * i, 2), c, h * ny + ys_at[src]]
            k = (1, 3)[i]
            yy.append((p, send(blk, blk, y_s.at[p, 0, k], y_r.at[p, 0, k],
                               dev(z, x, c, h, ys_at[to]))))
            yy[-1][1].start()

    for cp in a:
        cp.wait_recv()
    for p in range(order[1]):
        start_y(p, 0, ten)

    def spread_y(p):
        for n, cp in e:
            if n == p:
                cp.wait_recv()
        start_y(p, 1, toth)

    gc = [None] * pairs

    def to_core(p):
        for n, cp in yy:
            if n == p:
                cp.wait_recv()
        blk = gbuf.at[p, :, c]
        gc[p] = send(blk, blk, g_s.at[p], g_r.at[p], dev(z, x, oc, h, y))
        gc[p].start()

    h2 = []

    def on_x():
        for i, (k, src) in enumerate(((xr, xl), (xl, xr))):
            for cc in range(NC):
                send(hext.at[cc], hraw.at[src, cc], h_s.at[i, cc], h_r.at[i, cc],
                     dev(z, src, cc, h, y)).wait_recv()
                r0, rn = (0, split) if i == 0 else (split, hr - split)
                blk = hraw.at[src, cc, pl.ds(r0, rn)]
                h2.append(send(blk, blk, hf_s.at[i, cc], hf_r.at[i, cc],
                               dev(z, k, c, h, y)))
                h2[-1].start()

    def mask_rep(xs, cs):
        r = xs * NC + cs
        who = lang[z * (NX * NC) + r]
        at_col = pl.ds(pl.multiple_of(r * tok, tok), tok)
        val = hraw[xs, cs, :fh, :]
        for l in range(LANGS):
            keep = jnp.where(who == l, 1.0, 0.0).astype(F32)
            hm[l * fh:(l + 1) * fh, at_col] = (val * keep.astype(BF)).astype(BF)
        hm[LANGS * fh:, at_col] = hraw[xs, cs, fh:, :]

    def mask_near():
        hc.wait_recv()

        def some(i, carry):
            mask_rep(lax.rem(x + (NX - 1) + i // NC, NX), i % NC)
            return carry

        lax.fori_loop(0, (NX - 1) * NC, some, 0)

    def mask_far():
        for cp in h2:
            cp.wait_recv()
        for cs in range(NC):
            mask_rep(xs_at[2], cs)

    def pair(p):
        gc[p].wait_recv()
        right = gbuf[p].reshape(NX * NC * tok, 256)

        def some_rows(i, carry):
            r = pl.ds(pl.multiple_of(i * lp, lp), lp)
            res = jnp.dot(hm[r, :], right, preferred_element_type=F32).T
            part[nz - 1 - p, i] = res[:128]
            part[p, i] = res[128:]
            if p == 0:
                @pl.when(z == 0)
                def _():
                    chain_piece(0, nz - 1, i)

                @pl.when(z == nz - 1)
                def _():
                    chain_piece(1, 0, i)
            return carry

        lax.fori_loop(0, np_, some_rows, 0)

    def hop(way, o, q):
        return send(obuf.at[o, q], rbuf.at[way, o, q],
                    z_s.at[o, q], z_r.at[way, o, q],
                    dev(zn if way == 0 else zb, x, c, h, y))

    def last_hop(way, q, cc, o, cs):
        return send(obuf.at[o, q, pl.ds(64 * cc, 64)], fin.at[way, cs, q],
                    f_s.at[way, q, cc], f_r.at[way, q, cs],
                    dev(zn if way == 0 else zb, x, cc, h, y))

    def chain_piece(way, o, q):
        first = (z == 0) if way == 0 else (z == nz - 1)
        last = (o == z + 1) if way == 0 else (o == z - 1)

        @pl.when(jnp.logical_not(first))
        def _():
            hop(way, o, q).wait_recv()
            obuf[o, q] = (part[o, q] + rbuf[way, o, q].astype(F32)).astype(BF)

        @pl.when(first)
        def _():
            obuf[o, q] = part[o, q].astype(BF)

        @pl.when(last)
        def _():
            for cc in range(NC):
                last_hop(way, q, cc, o, c).start()

        @pl.when(jnp.logical_not(last))
        def _():
            hop(way, o, q).start()

    def slot(s):
        @pl.when(s >= z)
        def _():
            for q in range(np_):
                chain_piece(0, nz - 1 + z - s, q)

        @pl.when(s >= nz - 1 - z)
        def _():
            for q in range(np_):
                chain_piece(1, s - (nz - 1) + z, q)

    mine = pl.ds(pl.multiple_of(c * 64, 64), 64)
    other = pl.ds(pl.multiple_of(oc * 64, 64), 64)
    swap = send(part.at[z, :, other], sx, o_s.at[0], o_r.at[0], dev(z, x, oc, h, y))

    do = {"K": start_e, "Y": lambda p: start_y(p, 0, ten), "E": spread_y, "C": to_core, "X": on_x, "F": on_y, "M": mask_near, "N": mask_far,
          "P": pair, "S": slot, "W": swap.start}
    for step in [w for group in order[2:] for w in group.split()]:
        do[step[0]](*(int(v) for v in step[1:]))
    for s in range(max(pairs, 1), nz - 1):
        slot(s)

    for cp in a + h1 + [hc] + h2 + gc:
        cp.wait_send()
    for n, cp in e + yy + yo:
        cp.wait_send()

    swap.wait()
    low = c == 0
    writes = []
    for q in range(np_):
        one, two = part[z, q, mine, :], sx[q]
        acc[0, :, q * lp:(q + 1) * lp] = jnp.where(low, one, two)
        acc[1, :, q * lp:(q + 1) * lp] = jnp.where(low, two, one)
        for way, there in ((0, z > 0), (1, z < nz - 1)):
            @pl.when(there)
            def _():
                for cs in range(NC):
                    last_hop(way, q, cs, z, cs).wait_recv()
                    at_l = slice(q * lp, (q + 1) * lp)
                    acc[cs, :, at_l] = acc[cs, :, at_l] + fin[way, cs, q].astype(F32)

        for l in range(LANGS):
            if q * lp < (l + 1) * fh <= (q + 1) * lp:
                for cs in range(NC):
                    om[l, :, cs * fh:(cs + 1) * fh] = acc[cs, :, l * fh:(l + 1) * fh].astype(BF)
                writes.append(pltpu.make_async_copy(om.at[l], out_m.at[l], w_s.at[l]))
                writes[-1].start()
    for cs in range(NC):
        oa[:, cs * ch:(cs + 1) * ch] = acc[cs, :, LANGS * fh:]
    writes.append(pltpu.make_async_copy(oa, out_a, w_s.at[LANGS]))
    writes[-1].start()

    def drain(o, carry):
        @pl.when(jnp.logical_or(o > z + 1, o < z - 1))
        def _():
            for q in range(np_):
                hop(0, o, q).wait_send()
        return carry

    lax.fori_loop(0, nz, drain, 0)
    for q in range(np_):
        for way, there in ((0, z < nz - 1), (1, z > 0)):
            @pl.when(there)
            def _():
                for cc in range(NC):
                    last_hop(way, q, cc, z, c).wait_send()
    for cp in writes:
        cp.wait()


def shards(nz, ny, language, hidden, context, grad_out):
    tok, ff = hidden.shape
    nctx = context.shape[1]
    tt = grad_out.shape[0]
    fh, ch = ff // 2, nctx // 2
    hr, rows = fh + ch, LANGS * fh + ch
    np_ = 4 if rows % 512 == 0 else 3
    lp = rows // np_
    pairs = nz // 2
    dma = pltpu.SemaphoreType.DMA
    hbm = pl.BlockSpec(memory_space=pltpu.HBM)
    y1 = max(ny, 1)
    out_m, out_a = pl.pallas_call(
        functools.partial(body, nz, ny),
        out_shape=(jax.ShapeDtypeStruct((LANGS, 64, ff), BF),
                   jax.ShapeDtypeStruct((64, nctx), F32)),
        in_specs=[pl.BlockSpec(memory_space=pltpu.SMEM), hbm, hbm, hbm],
        out_specs=(hbm, hbm),
        scratch_shapes=[
            pltpu.VMEM((tt, nz * NX * 128), BF),
            pltpu.VMEM((tok, nctx), BF),
            pltpu.VMEM((pairs, NX, tt, 256), BF),
            pltpu.VMEM((NC, hr, tok), BF),
            pltpu.VMEM((NX, NC, hr, tok), BF),
            pltpu.VMEM((rows, NX * NC * tok), BF),
            pltpu.VMEM((pairs, NX, NC, NH * ny, tt, 256), BF),
            pltpu.VMEM((nz, np_, 128, lp), F32),
            pltpu.VMEM((2, nz, np_, 128, lp), BF),
            pltpu.VMEM((nz, np_, 128, lp), BF),
            pltpu.VMEM((2, NC, np_, 64, lp), BF),
            pltpu.VMEM((np_, 64, lp), F32),
            pltpu.VMEM((NC, 64, rows), F32),
            pltpu.VMEM((LANGS, 64, ff), BF),
            pltpu.VMEM((64, nctx), F32),
            dma((2 + NC,)),
            dma((NX - 1,)), dma((NX - 1,)),
            dma((pairs, NX)), dma((pairs, NX)),
            dma((2, NC)), dma((2, NC)), dma((2, NC)), dma((2, NC)),
            dma((1,)), dma((1,)),
            dma((pairs, 2, y1)), dma((pairs, 2, y1)),
            dma((pairs,)), dma((pairs,)),
            dma((nz, np_)), dma((2, nz, np_)),
            dma((2, np_, NC)), dma((2, np_, NC)),
            dma((1,)), dma((1,)),
            dma((1 + LANGS,)),
        ],
        compiler_params=pltpu.CompilerParams(
            collective_id=0, has_side_effects=True,
            vmem_limit_bytes=60 * 1024 * 1024),
        cost_estimate=pl.CostEstimate(
            flops=2 * rows * NX * NC * tok * nz * 128,
            bytes_accessed=4 * 1024 * 1024, transcendentals=0),
    )(language, hidden.T, context, grad_out)
    return jnp.swapaxes(out_m, 1, 2), out_a


def solution(mesh):
    nz = mesh.shape["dp"] // (NX * NC)
    ny = mesh.shape["tensor"] // NH
    return jax.shard_map(
        functools.partial(shards, nz, ny),
        mesh=mesh,
        in_specs=(P(), P("dp", "tensor"), P("dp", "tensor"), P(("dp", "tensor"), None)),
        out_specs=(P(None, "tensor", "dp"), P("dp", "tensor")),
        check_vma=False,
    )
```

```python
import functools

import jax
import jax.numpy as jnp
from jax import lax
from jax.experimental import pallas as pl
from jax.experimental.pallas import tpu as pltpu
from jax.sharding import PartitionSpec as P

LANGS = 4
NX = 4
NC = 2
NH = 2
BF = jnp.bfloat16
F32 = jnp.float32

ORDERS = {
    4: (4, 4, "F0 F1 F2 F3", "X M E0 E1", "C0 N E2 C1", "P0 E3 C2 P1", "S1 C3 P2 S2", "P3 W S3"),
    2: (1, 1, "E0 X K1 Y1", "C0 M N P0", "E1 C1 P1 W", "S1"),
    1: (1, 1, "E0 X C0 M", "N P0 W"),
}


def body(nz, ny, lang, hid, ctx, grad, out_m, out_a,
         graw, craw, own, hext, hraw, hm, gbuf, part, rbuf, obuf, fin, sx, acc, om, oa,
         l_s, a_s, a_r, e_s, e_r, h_s, h_r, hf_s, hf_r, hc_s, hc_r,
         y_s, y_r, g_s, g_r, z_s, z_r, f_s, f_r, o_s, o_r, w_s):
    ff, tok = hid.shape
    nctx = ctx.shape[1]
    fh, ch = ff // 2, nctx // 2
    hr = fh + ch
    np_, lp = part.shape[1], part.shape[3]
    pairs = nz // 2
    split = (hr // 32) * 16

    dp = lax.axis_index("dp")
    ten = lax.axis_index("tensor")
    z = dp // (NX * NC)
    x = (dp // NC) % NX
    c = dp % NC
    h = ten // ny
    y = ten % ny
    oc, oh = 1 - c, 1 - h
    toth = oh * ny + y

    def dev(z_, x_, c_, h_, y_):
        return ((z_ * NX + x_) * NC + c_, h_ * ny + y_)

    def send(src, dst, ssem, rsem, where):
        return pltpu.make_async_remote_copy(
            src_ref=src, dst_ref=dst, send_sem=ssem, recv_sem=rsem,
            device_id=where, device_id_type=pl.DeviceIdType.MESH)

    xs_at = [lax.rem(x + d, NX) for d in range(NX)]
    ys_at = [lax.rem(y + d, ny) for d in range(ny)]
    xr, xl = xs_at[1], xs_at[NX - 1]
    zn, zb = lax.rem(z + 1, nz), lax.rem(z + nz - 1, nz)

    loads = [pltpu.make_async_copy(grad, graw, l_s.at[0]),
             pltpu.make_async_copy(ctx, craw, l_s.at[1])]
    for k in range(NC):
        loads.append(pltpu.make_async_copy(
            hid.at[pl.ds(k * fh, fh)], hext.at[k, pl.ds(0, fh)], l_s.at[2 + k]))
    for cp in loads:
        cp.start()

    barrier = pltpu.get_barrier_semaphore()
    friends = [dev(z, k, c, h, y) for k in xs_at[1:]]
    friends += [dev(z, k, oc, h, y) for k in (x, xr, xl)]
    friends += [dev(z, k, c, oh, y) for k in xs_at]
    friends += [dev(z, x, c, h, k) for k in ys_at[1:]]
    friends += [dev(k, x, cc, h, y) for k in (zn, zb) for cc in range(NC)]
    for f in friends:
        pl.semaphore_signal(barrier, inc=1, device_id=f,
                            device_id_type=pl.DeviceIdType.MESH)

    loads[0].wait()
    for p in range(pairs):
        for k in range(NX):
            for i, o in enumerate((nz - 1 - p, p)):
                lo = (o * NX + k) * 128
                own[p, k, :, i * 128:(i + 1) * 128] = graw[:, lo:lo + 128]
    pl.semaphore_wait(barrier, len(friends))

    e, a, yy, yo = [], [], [], []

    def start_e(p):
        for d in range(NX):
            e.append((p, send(own.at[p, xs_at[d]], gbuf.at[p, x, c, ten],
                              e_s.at[p, d], e_r.at[p, d], dev(z, xs_at[d], c, oh, y))))
            e[-1][1].start()

    order = ORDERS[pairs]
    for p in range(order[0]):
        start_e(p)
    for d in range(1, NX):
        a.append(send(own.at[:, xs_at[d]], gbuf.at[:, x, c, ten],
                      a_s.at[d - 1], a_r.at[d - 1], dev(z, xs_at[d], c, h, y)))
        a[-1].start()
    loads[1].wait()
    ctx_t = craw[...].T
    for k in range(NC):
        hext[k, fh:, :] = ctx_t[k * ch:(k + 1) * ch, :]
    loads[2].wait()
    loads[3].wait()
    h1 = []
    for i, k in enumerate((xr, xl)):
        for cc in range(NC):
            h1.append(send(hext.at[cc], hraw.at[x, c],
                           h_s.at[i, cc], h_r.at[i, c], dev(z, k, cc, h, y)))
            h1[-1].start()
    hc = send(hext.at[oc], hraw.at[x, c], hc_s.at[0], hc_r.at[0],
              dev(z, x, oc, h, y))
    hc.start()
    gbuf[:, x, c, ten] = own[:, x]
    hraw[x, c] = hext[c]

    def start_y(p, w, t):
        blk = gbuf.at[p, :, c, t]
        for d in range(1, ny):
            if w == 0 and ny == 4 and d == 2:
                continue
            (yo if w == 0 and ny == 4 else yy).append((p, send(blk, blk, y_s.at[p, w, d - 1], y_r.at[p, w, d - 1],
                               dev(z, x, c, h, ys_at[d]))))
            (yo if w == 0 and ny == 4 else yy)[-1][1].start()

    def on_y(p):
        for n, cp in yo:
            if n == p:
                cp.wait_recv()
        for i, (to, src) in enumerate(((1, 3), (3, 1))):
            blk = gbuf.at[p, pl.ds(2 * i, 2), c, h * ny + ys_at[src]]
            k = (1, 3)[i]
            yy.append((p, send(blk, blk, y_s.at[p, 0, k], y_r.at[p, 0, k],
                               dev(z, x, c, h, ys_at[to]))))
            yy[-1][1].start()

    for cp in a:
        cp.wait_recv()
    for p in range(order[1]):
        start_y(p, 0, ten)

    def spread_y(p):
        for n, cp in e:
            if n == p:
                cp.wait_recv()
        start_y(p, 1, toth)

    gc = [None] * pairs

    def to_core(p):
        for n, cp in yy:
            if n == p:
                cp.wait_recv()
        blk = gbuf.at[p, :, c]
        gc[p] = send(blk, blk, g_s.at[p], g_r.at[p], dev(z, x, oc, h, y))
        gc[p].start()

    h2 = []

    def on_x():
        for i, (k, src) in enumerate(((xr, xl), (xl, xr))):
            for cc in range(NC):
                send(hext.at[cc], hraw.at[src, cc], h_s.at[i, cc], h_r.at[i, cc],
                     dev(z, src, cc, h, y)).wait_recv()
                r0, rn = (0, split) if i == 0 else (split, hr - split)
                blk = hraw.at[src, cc, pl.ds(r0, rn)]
                h2.append(send(blk, blk, hf_s.at[i, cc], hf_r.at[i, cc],
                               dev(z, k, c, h, y)))
                h2[-1].start()

    def mask_rep(xs, cs):
        r = xs * NC + cs
        who = lang[z * (NX * NC) + r]
        at_col = pl.ds(pl.multiple_of(r * tok, tok), tok)
        val = hraw[xs, cs, :fh, :]
        for l in range(LANGS):
            keep = jnp.where(who == l, 1.0, 0.0).astype(F32)
            hm[l * fh:(l + 1) * fh, at_col] = (val * keep.astype(BF)).astype(BF)
        hm[LANGS * fh:, at_col] = hraw[xs, cs, fh:, :]

    def mask_near():
        hc.wait_recv()

        def some(i, carry):
            mask_rep(lax.rem(x + (NX - 1) + i // NC, NX), i % NC)
            return carry

        lax.fori_loop(0, (NX - 1) * NC, some, 0)

    def mask_far():
        for cp in h2:
            cp.wait_recv()
        for cs in range(NC):
            mask_rep(xs_at[2], cs)

    def pair(p):
        gc[p].wait_recv()
        right = gbuf[p].reshape(NX * NC * tok, 256)

        def some_rows(i, carry):
            r = pl.ds(pl.multiple_of(i * lp, lp), lp)
            res = jnp.dot(hm[r, :], right, preferred_element_type=F32).T
            part[nz - 1 - p, i] = res[:128]
            part[p, i] = res[128:]

            @pl.when(z == 0)
            def _():
                chain_piece(0, nz - 1 - p, i)

            @pl.when(z == nz - 1)
            def _():
                chain_piece(1, p, i)

            return carry

        lax.fori_loop(0, np_, some_rows, 0)

    def hop(way, o, q):
        return send(obuf.at[o, q], rbuf.at[way, o, q],
                    z_s.at[o, q], z_r.at[way, o, q],
                    dev(zn if way == 0 else zb, x, c, h, y))

    def last_hop(way, q, cc, o, cs):
        return send(obuf.at[o, q, pl.ds(64 * cc, 64)], fin.at[way, cs, q],
                    f_s.at[way, q, cc], f_r.at[way, q, cs],
                    dev(zn if way == 0 else zb, x, cc, h, y))

    def chain_piece(way, o, q):
        first = (z == 0) if way == 0 else (z == nz - 1)
        last = (o == z + 1) if way == 0 else (o == z - 1)

        @pl.when(jnp.logical_not(first))
        def _():
            hop(way, o, q).wait_recv()
            obuf[o, q] = (part[o, q] + rbuf[way, o, q].astype(F32)).astype(BF)

        @pl.when(first)
        def _():
            obuf[o, q] = part[o, q].astype(BF)

        @pl.when(last)
        def _():
            for cc in range(NC):
                last_hop(way, q, cc, o, c).start()

        @pl.when(jnp.logical_not(last))
        def _():
            hop(way, o, q).start()

    def slot(s):
        inner = jnp.logical_or(s >= pairs, jnp.logical_and(z > 0, z < nz - 1))

        @pl.when(jnp.logical_and(s >= z, inner))
        def _():
            for q in range(np_):
                chain_piece(0, nz - 1 + z - s, q)

        @pl.when(jnp.logical_and(s >= nz - 1 - z, inner))
        def _():
            for q in range(np_):
                chain_piece(1, s - (nz - 1) + z, q)

    mine = pl.ds(pl.multiple_of(c * 64, 64), 64)
    other = pl.ds(pl.multiple_of(oc * 64, 64), 64)
    swap = send(part.at[z, :, other], sx, o_s.at[0], o_r.at[0], dev(z, x, oc, h, y))

    do = {"K": start_e, "Y": lambda p: start_y(p, 0, ten), "E": spread_y, "C": to_core, "X": on_x, "F": on_y, "M": mask_near, "N": mask_far,
          "P": pair, "S": slot, "W": swap.start}
    for step in [w for group in order[2:] for w in group.split()]:
        do[step[0]](*(int(v) for v in step[1:]))
    for s in range(max(pairs, 1), nz - 1):
        slot(s)

    for cp in a + h1 + [hc] + h2 + gc:
        cp.wait_send()
    for n, cp in e + yy + yo:
        cp.wait_send()

    swap.wait()
    low = c == 0
    writes = []
    for q in range(np_):
        one, two = part[z, q, mine, :], sx[q]
        acc[0, :, q * lp:(q + 1) * lp] = jnp.where(low, one, two)
        acc[1, :, q * lp:(q + 1) * lp] = jnp.where(low, two, one)
        for way, there in ((0, z > 0), (1, z < nz - 1)):
            @pl.when(there)
            def _():
                for cs in range(NC):
                    last_hop(way, q, cs, z, cs).wait_recv()
                    at_l = slice(q * lp, (q + 1) * lp)
                    acc[cs, :, at_l] = acc[cs, :, at_l] + fin[way, cs, q].astype(F32)

        for l in range(LANGS):
            if q * lp < (l + 1) * fh <= (q + 1) * lp:
                for cs in range(NC):
                    om[l, :, cs * fh:(cs + 1) * fh] = acc[cs, :, l * fh:(l + 1) * fh].astype(BF)
                writes.append(pltpu.make_async_copy(om.at[l], out_m.at[l], w_s.at[l]))
                writes[-1].start()
    for cs in range(NC):
        oa[:, cs * ch:(cs + 1) * ch] = acc[cs, :, LANGS * fh:]
    writes.append(pltpu.make_async_copy(oa, out_a, w_s.at[LANGS]))
    writes[-1].start()

    def drain(o, carry):
        @pl.when(jnp.logical_or(o > z + 1, o < z - 1))
        def _():
            for q in range(np_):
                hop(0, o, q).wait_send()
        return carry

    lax.fori_loop(0, nz, drain, 0)
    for q in range(np_):
        for way, there in ((0, z < nz - 1), (1, z > 0)):
            @pl.when(there)
            def _():
                for cc in range(NC):
                    last_hop(way, q, cc, z, c).wait_send()
    for cp in writes:
        cp.wait()


def shards(nz, ny, language, hidden, context, grad_out):
    tok, ff = hidden.shape
    nctx = context.shape[1]
    tt = grad_out.shape[0]
    fh, ch = ff // 2, nctx // 2
    hr, rows = fh + ch, LANGS * fh + ch
    np_ = 4 if rows % 512 == 0 else 3
    lp = rows // np_
    pairs = nz // 2
    dma = pltpu.SemaphoreType.DMA
    hbm = pl.BlockSpec(memory_space=pltpu.HBM)
    y1 = max(ny, 1)
    out_m, out_a = pl.pallas_call(
        functools.partial(body, nz, ny),
        out_shape=(jax.ShapeDtypeStruct((LANGS, 64, ff), BF),
                   jax.ShapeDtypeStruct((64, nctx), F32)),
        in_specs=[pl.BlockSpec(memory_space=pltpu.SMEM), hbm, hbm, hbm],
        out_specs=(hbm, hbm),
        scratch_shapes=[
            pltpu.VMEM((tt, nz * NX * 128), BF),
            pltpu.VMEM((tok, nctx), BF),
            pltpu.VMEM((pairs, NX, tt, 256), BF),
            pltpu.VMEM((NC, hr, tok), BF),
            pltpu.VMEM((NX, NC, hr, tok), BF),
            pltpu.VMEM((rows, NX * NC * tok), BF),
            pltpu.VMEM((pairs, NX, NC, NH * ny, tt, 256), BF),
            pltpu.VMEM((nz, np_, 128, lp), F32),
            pltpu.VMEM((2, nz, np_, 128, lp), BF),
            pltpu.VMEM((nz, np_, 128, lp), BF),
            pltpu.VMEM((2, NC, np_, 64, lp), BF),
            pltpu.VMEM((np_, 64, lp), F32),
            pltpu.VMEM((NC, 64, rows), F32),
            pltpu.VMEM((LANGS, 64, ff), BF),
            pltpu.VMEM((64, nctx), F32),
            dma((2 + NC,)),
            dma((NX - 1,)), dma((NX - 1,)),
            dma((pairs, NX)), dma((pairs, NX)),
            dma((2, NC)), dma((2, NC)), dma((2, NC)), dma((2, NC)),
            dma((1,)), dma((1,)),
            dma((pairs, 2, y1)), dma((pairs, 2, y1)),
            dma((pairs,)), dma((pairs,)),
            dma((nz, np_)), dma((2, nz, np_)),
            dma((2, np_, NC)), dma((2, np_, NC)),
            dma((1,)), dma((1,)),
            dma((1 + LANGS,)),
        ],
        compiler_params=pltpu.CompilerParams(
            collective_id=0, has_side_effects=True,
            vmem_limit_bytes=60 * 1024 * 1024),
        cost_estimate=pl.CostEstimate(
            flops=2 * rows * NX * NC * tok * nz * 128,
            bytes_accessed=4 * 1024 * 1024, transcendentals=0),
    )(language, hidden.T, context, grad_out)
    return jnp.swapaxes(out_m, 1, 2), out_a


def solution(mesh):
    nz = mesh.shape["dp"] // (NX * NC)
    ny = mesh.shape["tensor"] // NH
    return jax.shard_map(
        functools.partial(shards, nz, ny),
        mesh=mesh,
        in_specs=(P(), P("dp", "tensor"), P("dp", "tensor"), P(("dp", "tensor"), None)),
        out_specs=(P(None, "tensor", "dp"), P("dp", "tensor")),
        check_vma=False,
    )
```
